256 devices in a mesh: grp: 8 (over x_hi, y), dev: 32 (over x_lo, z, core).
Axes of the slice: x: 4 (x_hi: 2, x_lo: 2; x = x_hi * 2 + x_lo), y: 4, z: 8, core: 2. Of those that a mesh axis runs over, the one named last changes fastest.
Arguments:
- state: float32 [8, 32, 524288], P('grp', 'dev'), may hold values from -6 to 6
- angles: float32 [2, 27], replicated, may hold values from -3.140625 to 3.140625
Outputs:
- evolved: float32 [8, 32, 524288], P('grp', 'dev')
The draws below stay inside these ranges and needn't reach their ends.
All inputs are finite; a program needn't handle non-finite values.
Results may differ from the reference program's by a relative error of at most 0.00014.
Values sent between devices are 32-bit elements; how exact they have to be, the bound alone decides.
A program may use at most 192 MiB of HBM per device.

```python
import jax
import jax.numpy as jnp
from jax import lax

AMP_DEV = 524288
LAYERS = 2
NQ = 27
N_GRP = 8
N_DEV = 32


def steps_of(own_key, extent, split, smallest, high):
    loudness, own = 1.0, jax.random.fold_in(own_key, 6)
    for dim, parts in split:
        draws = jnp.exp(jax.random.uniform(jax.random.fold_in(own, dim), (parts,), jnp.float32, smallest / len(split), high / len(split)))
        loudness = loudness * jnp.repeat(draws, extent[dim] // parts).reshape([-1 if axis == dim else 1 for axis in range(len(extent))])
    return loudness


def centred(own_key, extent, width, bound, split=(), kind=jnp.bfloat16):
    result = width * jax.random.normal(own_key, extent, jnp.float32)
    if split:
        result = result * steps_of(own_key, extent, split, -0.22, 0.18)
    return jnp.clip(result, -bound, bound).astype(kind)


def setup_inputs(seed: int = 0) -> dict:
    keys = jax.random.split(jax.random.key(seed), 3)
    state = centred(keys[0], (N_GRP, N_DEV, AMP_DEV), 1.0, 6.0, ((0, 8), (1, 32)), jnp.float32)
    angles = jnp.clip(jax.random.uniform(keys[1], (LAYERS, NQ), jnp.float32, -3.140625, 3.140625), -3.140625, 3.140625)
    return {"state": state, "angles": angles}


HIGH = lax.Precision.HIGHEST


def ladder(values, nbits):
    total = jnp.zeros_like(values)
    for j in range(nbits - 1):
        total = total + ((values >> j) & (values >> (j + 1)) & 1)
    return total % 2


def joined_gate(slot_angles):
    index = jnp.arange(128, dtype=jnp.int32)
    rows = index[:, None]
    cols = index[None, :]
    matrix = jnp.ones((128, 128), slot_angles.dtype)
    for j in range(7):
        cosine = jnp.cos(0.5 * slot_angles[j])
        sine = jnp.sin(0.5 * slot_angles[j])
        row_bit = (rows >> j) & 1
        col_bit = (cols >> j) & 1
        entry = jnp.where(row_bit == col_bit, cosine, jnp.where(row_bit == 1, sine, -sine))
        matrix = matrix * entry
    return matrix


def gate_plan(local_bits, dev_bits, grp_bits):
    claimed_qubits = []

    def claim(wanted):
        chosen_slots = []
        for qubit_id in wanted:
            if qubit_id in claimed_qubits:
                chosen_slots.append(-1)
            else:
                claimed_qubits.append(qubit_id)
                chosen_slots.append(qubit_id)
        return chosen_slots

    grp_slots = claim(list(range(7 - grp_bits)) + [local_bits + dev_bits + j for j in range(grp_bits)])
    dev_slots = claim([local_bits - 7 + j for j in range(7 - dev_bits)] + [local_bits + j for j in range(dev_bits)])
    offsets = list(range(0, local_bits - 6, 7))
    if offsets[-1] + 7 < local_bits:
        offsets.append(local_bits - 7)
    windows = []
    for offset in offsets:
        slot_list = claim(list(range(offset, offset + 7)))
        if max(slot_list) >= 0:
            windows.append((offset, slot_list))
    return windows, dev_slots, grp_slots


def slot_gate(angles, layer, slot_list):
    picked = [angles[layer, k] if k >= 0 else jnp.zeros((), angles.dtype) for k in slot_list]
    return joined_gate(jnp.stack(picked))


def apply_window(flat, gate, offset):
    if offset == 0:
        return jnp.dot(flat.reshape(-1, 128), gate.T, precision=HIGH).reshape(-1)
    shaped = flat.reshape(-1, 128, 2 ** offset)
    return jnp.einsum('ab,ibk->iak', gate, shaped, precision=HIGH).reshape(-1)


def reference(state, angles):
    n_grp = N_GRP
    n_dev = N_DEV
    amp = AMP_DEV
    local_bits = amp.bit_length() - 1
    dev_bits = n_dev.bit_length() - 1
    grp_bits = n_grp.bit_length() - 1
    upper = amp // 128
    windows, dev_slots, grp_slots = gate_plan(local_bits, dev_bits, grp_bits)
    device = jnp.arange(n_grp * n_dev, dtype=jnp.int32)
    high_idx = jnp.arange(upper, dtype=jnp.int32)
    low_idx = jnp.arange(128, dtype=jnp.int32)
    local_par = ladder(high_idx, local_bits - 7)[:, None] + ladder(low_idx, 7)[None, :]
    local_par = local_par + (high_idx & 1)[:, None] * ((low_idx >> 6) & 1)[None, :]
    top_bit = (high_idx >> (local_bits - 8)) & 1
    parity = ladder(device, dev_bits + grp_bits)[:, None, None] + local_par[None, :, :]
    parity = (parity + top_bit[None, :, None] * (device & 1)[:, None, None]) % 2
    signs = (1 - 2 * parity).astype(state.dtype).reshape(-1)
    x = state.reshape(-1)
    for layer in range(LAYERS):
        for offset, slot_list in windows:
            x = apply_window(x, slot_gate(angles, layer, slot_list), offset)
        mid = 2 ** (7 - dev_bits)
        u_dev = slot_gate(angles, layer, dev_slots).reshape(n_dev, mid, n_dev, mid)
        x = jnp.einsum('abcd,gcxdl->gaxbl', u_dev, x.reshape(n_grp, n_dev, n_dev, mid, upper), precision=HIGH)
        low = 2 ** (7 - grp_bits)
        u_grp = slot_gate(angles, layer, grp_slots).reshape(n_grp, low, n_grp, low)
        x = jnp.einsum('abcd,cymd->aymb', u_grp, x.reshape(n_grp, -1, n_grp, low), precision=HIGH)
        x = x.reshape(-1) * signs
    return x.reshape(N_GRP, N_DEV, AMP_DEV)
```

```python
import jax
import jax.numpy as jnp
from jax import lax
from jax.experimental import pallas as pl
from jax.experimental.pallas import tpu as pltpu
from jax.sharding import PartitionSpec as P

MESH = pl.DeviceIdType.MESH
F32, BF16 = jnp.float32, jnp.bfloat16
W_QUBITS = (19, 23, 24, 25, 26)
BW_QUBITS = (11, 12, 13, 14, 15)
ROW_QUBITS = (7, 8, 9) + W_QUBITS
COL_QUBITS = (0, 1, 2, 3, 4, 5, 6, 20)
QUARTERS = 4


def rotate(tiles, bit, gate):
    cosine, sine = gate
    out = list(tiles)
    for i in range(len(tiles)):
        if not i >> bit & 1:
            j = i | 1 << bit
            out[i] = cosine * tiles[i] - sine * tiles[j]
            out[j] = sine * tiles[i] + cosine * tiles[j]
    return out


def ladder(values, nbits):
    total = values & values >> 1
    parity = total & 1
    for j in range(1, nbits - 1):
        parity = parity + (total >> j & 1)
    return parity


def signs(parity):
    return (1 - 2 * (parity & 1)).astype(F32)


def split(value):
    high = value.astype(BF16)
    return high, (value - high.astype(F32)).astype(BF16)


def dot3(a, b):
    return (
        jnp.dot(a[0], b[0], preferred_element_type=F32)
        + jnp.dot(a[0], b[1], preferred_element_type=F32)
        + jnp.dot(a[1], b[0], preferred_element_type=F32)
    )


def kernel(
    state, angles, out,
    x, p_buf, q_buf, q2, w_buf, m_buf, v_buf, v2, t_buf, o_buf, ys, cz, gate_hi, gate_lo,
    load_sem, store_sem, fz_s, fz_r, fw_s, fw_r, bw_s, bw_r, bz_s, bz_r, last_s, last_r,
):
    grp, dev = lax.axis_index("grp"), lax.axis_index("dev")
    core, my_z, x_lo = lax.rem(dev, 2), lax.rem(lax.div(dev, 2), 8), lax.div(dev, 16)
    my_w = core + 2 * x_lo + 4 * grp
    my_p, my_h = lax.rem(my_z, 2), lax.div(my_z, 2)

    def z_device(z):
        return (grp, 16 * x_lo + 2 * z + core)

    def w_device(w):
        return (lax.div(w, 4), 16 * lax.rem(lax.div(w, 2), 2) + 2 * my_z + lax.rem(w, 2))

    def other_w(k):
        return lax.rem(my_w + k, 32)

    def load(i):
        part = pl.ds(8 * i, 8)
        return pltpu.make_async_copy(state.at[:, part], x.at[:, part], load_sem.at[i])

    def store(i):
        part = pl.ds(8 * i, 8)
        return pltpu.make_async_copy(o_buf.at[:, part], out.at[:, part], store_sem.at[i])

    for i in range(QUARTERS):
        load(i).start()
    barrier = pltpu.get_barrier_semaphore()

    @pl.loop(1, 8)
    def _(k):
        pl.semaphore_signal(barrier, inc=1, device_id=z_device(lax.rem(my_z + k, 8)), device_id_type=MESH)

    @pl.loop(1, 32)
    def _(k):
        pl.semaphore_signal(barrier, inc=1, device_id=w_device(other_w(k)), device_id_type=MESH)

    half = 0.5 * angles[...]
    cosines, sines = jnp.cos(half), jnp.sin(half)

    def gate(layer, qubit, shape=(8, 128)):
        at = (slice(layer, layer + 1), slice(qubit, qubit + 1))
        return jnp.broadcast_to(cosines[at], shape), jnp.broadcast_to(sines[at], shape)

    first = [gate(0, q) for q in (10, 16, 17, 18)]
    for i in range(QUARTERS):
        load(i).wait()

        @pl.loop(8 * i, 8 * i + 8)
        def _(bw):
            tiles = [x[j >> 1, bw, j & 1] for j in range(16)]
            for bit in range(4):
                tiles = rotate(tiles, bit, first[bit])
            for j in range(16):
                z = j >> 1
                p_buf[j & 1, z & 1, z >> 1, bw] = tiles[j]

    pl.semaphore_wait(barrier, 38)

    def send_z(source, target, c, g, send_sem, recv_sem):
        def one(h, p):
            pltpu.make_async_remote_copy(
                src_ref=source.at[c, p, h], dst_ref=target.at[c, my_p, my_h],
                send_sem=send_sem.at[c, g], recv_sem=recv_sem.at[c, g],
                device_id=z_device(2 * h + p), device_id_type=MESH,
            ).start()

        if g == 0:
            @pl.loop(0, 4)
            def _(k):
                one(lax.rem(my_h + k, 4), 1 - my_p)
        else:
            @pl.loop(1, 4)
            def _(k):
                one(lax.rem(my_h + k, 4), my_p)

    def wait_z(buffer, c, g, sem):
        part = buffer.at[c, 1 - my_p] if g == 0 else buffer.at[c, my_p, pl.ds(0, 3)]
        pltpu.make_async_copy(part, part, sem.at[c, g]).wait()

    def send_w(source, target, c, g, send_sem, recv_sem):
        p = 1 - my_p if g == 0 else my_p

        @pl.loop(1, 32)
        def _(k):
            w = other_w(k)
            pltpu.make_async_remote_copy(
                src_ref=source.at[c, w, p], dst_ref=target.at[c, my_w, p],
                send_sem=send_sem.at[c, g], recv_sem=recv_sem.at[c, g],
                device_id=w_device(w), device_id_type=MESH,
            ).start()

        target[c, my_w, p] = source[c, my_w, p]

    def wait_w(buffer, c, g, sem):
        part = buffer.at[c, pl.ds(0, 31), 0]
        pltpu.make_async_copy(part, part, sem.at[c, g]).wait()

    send_z(p_buf, q_buf, 0, 0, fz_s, fz_r)
    send_z(p_buf, q_buf, 0, 1, fz_s, fz_r)

    for c in range(2):
        q_buf[c, my_p, my_h] = p_buf[c, my_p, my_h]

    square = (256, 256)
    rows = lax.broadcasted_iota(jnp.int32, square, 0)
    cols = lax.broadcasted_iota(jnp.int32, square, 1)
    for layer in range(2):
        for side, qubits in enumerate((ROW_QUBITS, COL_QUBITS)):
            matrix = None
            for j, q in enumerate(qubits):
                cosine, sine = gate(layer, q, square)
                to, of = (rows, cols) if side == 0 else (cols, rows)
                a, b = to >> j & 1, of >> j & 1
                entry = jnp.where(a == b, cosine, jnp.where(a == 1, sine, -sine))
                matrix = entry if matrix is None else matrix * entry
            gate_hi[layer, side], gate_lo[layer, side] = split(matrix)

    w_row, p_col = rows >> 3, cols >> 7
    fixed = ladder(my_w, 5) + ladder(my_z, 3) + (my_w >> 4 & my_z & 1)
    cross = (
        ladder(cols & 127, 7) + (cols >> 6 & rows & 1) + ladder(rows & 7, 3) + (my_z >> 2 & w_row & 1)
        + (w_row & p_col & 1) + ladder(w_row >> 1, 4) + fixed
    )
    for h in range(4):
        with_h = cross + (p_col & h & 1) + (h >> 1 & w_row >> 1 & 1) + (h & h >> 1 & 1)
        cz[0, h] = signs(with_h)
        cz[1, h] = signs(with_h + (rows >> 2 & 1) + (my_w & 1))

    def rotate_bw(source, target, c, p, layer, forward):
        gates = [gate(layer, q) for q in BW_QUBITS]

        @pl.loop(0, 4)
        def _(h):
            tiles = [source[c, p, h, w] if forward else source[c, w, p, h] for w in range(32)]
            for bit in range(5):
                tiles = rotate(tiles, bit, gates[bit])
            for w in range(32):
                if forward:
                    target[c, w, p, h] = tiles[w]
                else:
                    target[c, p, h, w] = tiles[w]

    h_gates = [[gate(layer, q, (8, 256)) for q in (21, 22)] for layer in range(2)]

    def middle(c):
        def both_sides(layer, block):
            left = (gate_hi[layer, 0], gate_lo[layer, 0])
            right = (gate_hi[layer, 1], gate_lo[layer, 1])
            return dot3(split(dot3(left, split(block))), right)

        @pl.loop(0, 4)
        def _(h):
            block = jnp.concatenate([w_buf[c, :, p, h].reshape(256, 128) for p in range(2)], axis=1)
            ys[h] = both_sides(0, block)

        @pl.loop(0, 32)
        def _(r):
            part = pl.ds(pl.multiple_of(8 * r, 8), 8)
            tiles = [ys[h, part] for h in range(4)]
            for layer in range(2):
                for bit in range(2):
                    tiles = rotate(tiles, bit, h_gates[layer][bit])
                if layer == 0:
                    tiles = [tiles[h] * cz[c, h, part] for h in range(4)]
            for h in range(4):
                ys[h, part] = tiles[h]

        @pl.loop(0, 4)
        def _(h):
            block = both_sides(1, ys[h])
            for p in range(2):
                m_buf[c, :, p, h] = block[:, 128 * p:128 * p + 128].reshape(32, 8, 128)

    def forward_z(c, g):
        wait_z(q_buf, c, g, fz_r)
        if c == 0:
            send_z(p_buf, q_buf, 1, g, fz_s, fz_r)
        rotate_bw(q_buf, q2, c, 1 - my_p if g == 0 else my_p, 0, True)
        send_w(q2, w_buf, c, g, fw_s, fw_r)

    def forward_w(c):
        for g in range(2):
            wait_w(w_buf, c, g, fw_r)
        middle(c)
        for g in range(2):
            send_w(m_buf, v_buf, c, g, bw_s, bw_r)

    def backward_w(c, g):
        wait_w(v_buf, c, g, bw_r)
        rotate_bw(v_buf, v2, c, 1 - my_p if g == 0 else my_p, 1, False)
        if c == 0 or g == 0:
            send_z(v2, t_buf, c, g, bz_s, bz_r)
        else:
            for i in range(QUARTERS):
                part = pl.ds(8 * i, 8)

                @pl.loop(1, 4)
                def _(k):
                    h = lax.rem(my_h + k, 4)
                    pltpu.make_async_remote_copy(
                        src_ref=v2.at[c, my_p, h, part], dst_ref=t_buf.at[c, my_p, my_h, part],
                        send_sem=last_s.at[i], recv_sem=last_r.at[i],
                        device_id=z_device(2 * h + my_p), device_id_type=MESH,
                    ).start()
        if g == 1:
            t_buf[c, my_p, my_h] = v2[c, my_p, my_h]

    forward_z(0, 0)
    forward_z(0, 1)
    forward_w(0)
    forward_z(1, 0)
    backward_w(0, 0)
    forward_z(1, 1)
    backward_w(0, 1)
    forward_w(1)
    backward_w(1, 0)
    backward_w(1, 1)

    second = [gate(1, q) for q in (10, 16, 17, 18)]
    sub = lax.broadcasted_iota(jnp.int32, (8, 128), 0)
    lane = lax.broadcasted_iota(jnp.int32, (8, 128), 1)
    base = ladder(lane, 7) + (lane >> 6 & sub & 1) + ladder(sub, 3)
    base = base + ladder(dev, 5) + ladder(grp, 3) + (dev >> 4 & grp & 1)
    tile_signs = [signs(base + c * (sub >> 2 & 1)) for c in range(2)]
    for c, g in ((0, 0), (0, 1), (1, 0)):
        wait_z(t_buf, c, g, bz_r)
    for i in range(QUARTERS):
        part = t_buf.at[1, 0, pl.ds(0, 3), pl.ds(8 * i, 8)]
        pltpu.make_async_copy(part, part, last_r.at[i]).wait()

        @pl.loop(8 * i, 8 * i + 8)
        def _(bw):
            tiles = [t_buf[j & 1, j >> 1 & 1, j >> 2, bw] for j in range(16)]
            for bit in range(4):
                tiles = rotate(tiles, bit, second[bit])
            for j in range(16):
                c, z = j & 1, j >> 1
                parity = ladder(bw, 5) + (c & bw & 1) + (bw >> 4 & z & 1) + (z >> 2 & core & 1)
                parity = parity + (z & z >> 1 & 1) + (z >> 1 & z >> 2 & 1)
                o_buf[z, bw, c] = tiles[j] * (tile_signs[c] * signs(parity))

        store(i).start()

    for c in range(2):
        for g in range(2):
            wait_z(p_buf, c, g, fz_s)
            wait_w(q2, c, g, fw_s)
            wait_w(m_buf, c, g, bw_s)
            if c == 0 or g == 0:
                wait_z(v2, c, g, bz_s)
    for i in range(QUARTERS):
        part = v2.at[1, 0, pl.ds(0, 3), pl.ds(8 * i, 8)]
        pltpu.make_async_copy(part, part, last_s.at[i]).wait()
        store(i).wait()


def shards(state, angles):
    view = (8, 32, 2, 8, 128)
    by_z = (2, 2, 4, 32, 8, 128)
    by_w = (2, 32, 2, 4, 8, 128)
    pairs = pltpu.SemaphoreType.DMA((2, 2))
    quarters = pltpu.SemaphoreType.DMA((QUARTERS,))
    out = pl.pallas_call(
        kernel,
        out_shape=jax.ShapeDtypeStruct(view, F32),
        in_specs=[pl.BlockSpec(memory_space=pl.ANY), pl.BlockSpec(memory_space=pltpu.VMEM)],
        out_specs=pl.BlockSpec(memory_space=pl.ANY),
        scratch_shapes=[
            pltpu.VMEM(view, F32),
            pltpu.VMEM(by_z, F32), pltpu.VMEM(by_z, F32),
            pltpu.VMEM(by_w, F32), pltpu.VMEM(by_w, F32), pltpu.VMEM(by_w, F32), pltpu.VMEM(by_w, F32),
            pltpu.VMEM(by_z, F32), pltpu.VMEM(by_z, F32),
            pltpu.VMEM(view, F32),
            pltpu.VMEM((4, 256, 256), F32),
            pltpu.VMEM((2, 4, 256, 256), F32),
            pltpu.VMEM((2, 2, 256, 256), BF16), pltpu.VMEM((2, 2, 256, 256), BF16),
            quarters, quarters,
            pairs, pairs, pairs, pairs, pairs, pairs, pairs, pairs,
            quarters, quarters,
        ],
        compiler_params=pltpu.CompilerParams(
            collective_id=0, has_side_effects=True, vmem_limit_bytes=48 * 2**20
        ),
    )(state.reshape(view), angles)
    return out.reshape(state.shape)


def solution(mesh):
    placed = (P("grp", "dev", None), P())
    return jax.shard_map(
        shards, mesh=mesh, in_specs=placed, out_specs=P("grp", "dev", None), check_vma=False
    )
```

```python
import jax
import jax.numpy as jnp
from jax import lax
from jax.experimental import pallas as pl
from jax.experimental.pallas import tpu as pltpu
from jax.sharding import PartitionSpec as P

MESH = pl.DeviceIdType.MESH
F32, BF16 = jnp.float32, jnp.bfloat16
W_QUBITS = (19, 23, 24, 25, 26)
BW_QUBITS = (11, 12, 13, 14, 15)
ROW_QUBITS = (7, 8, 9) + W_QUBITS
COL_QUBITS = (0, 1, 2, 3, 4, 5, 6, 20)
QUARTERS = 4


def rotate(tiles, bit, gate):
    cosine, sine = gate
    out = list(tiles)
    for i in range(len(tiles)):
        if not i >> bit & 1:
            j = i | 1 << bit
            out[i] = cosine * tiles[i] - sine * tiles[j]
            out[j] = sine * tiles[i] + cosine * tiles[j]
    return out


def ladder(values, nbits):
    total = values & values >> 1
    parity = total & 1
    for j in range(1, nbits - 1):
        parity = parity + (total >> j & 1)
    return parity


def signs(parity):
    return (1 - 2 * (parity & 1)).astype(F32)


def split(value):
    high = value.astype(BF16)
    return high, (value - high.astype(F32)).astype(BF16)


def dot3(a, b):
    return (
        jnp.dot(a[0], b[0], preferred_element_type=F32)
        + jnp.dot(a[0], b[1], preferred_element_type=F32)
        + jnp.dot(a[1], b[0], preferred_element_type=F32)
    )


def kernel(
    state, angles, out,
    x, turns, p_buf, q_buf, w_buf, m_buf, v_buf, t_buf, ys, cz, gate_left, gate_right,
    load_sem, turns_sem, fz_s, fz_r, fw_s, fw_r, bw_s, bw_r, bz_s, bz_r, last_s, last_r,
):
    grp, dev = lax.axis_index("grp"), lax.axis_index("dev")
    core, my_z, x_lo = lax.rem(dev, 2), lax.rem(lax.div(dev, 2), 8), lax.div(dev, 16)
    my_w = core + 2 * x_lo + 4 * grp
    my_p, my_h = lax.rem(my_z, 2), lax.div(my_z, 2)

    def z_device(z):
        return (grp, 16 * x_lo + 2 * z + core)

    def w_device(w):
        return (lax.div(w, 4), 16 * lax.rem(lax.div(w, 2), 2) + 2 * my_z + lax.rem(w, 2))

    def other_w(k):
        return lax.rem(my_w + k, 32)

    def load(i):
        part = pl.ds(8 * i, 8)
        return pltpu.make_async_copy(state.at[:, part], x.at[:, part], load_sem.at[i])

    load_turns = pltpu.make_async_copy(angles, turns, turns_sem)
    load_turns.start()
    for i in range(QUARTERS):
        load(i).start()
    barrier = pltpu.get_barrier_semaphore()

    @pl.loop(1, 8)
    def _(k):
        pl.semaphore_signal(barrier, inc=1, device_id=z_device(lax.rem(my_z + k, 8)), device_id_type=MESH)

    @pl.loop(1, 32)
    def _(k):
        pl.semaphore_signal(barrier, inc=1, device_id=w_device(other_w(k)), device_id_type=MESH)

    load_turns.wait()
    half = 0.5 * turns[...]
    cosines, sines = jnp.cos(half), jnp.sin(half)

    def gate(layer, qubit, shape=(8, 128)):
        at = (slice(layer, layer + 1), slice(qubit, qubit + 1))
        return jnp.broadcast_to(cosines[at], shape), jnp.broadcast_to(sines[at], shape)

    first = [gate(0, q) for q in (10, 16, 17, 18)]
    for i in range(QUARTERS):
        load(i).wait()

        @pl.loop(8 * i, 8 * i + 8)
        def _(bw):
            tiles = [x[j >> 1, bw, j & 1] for j in range(16)]
            for bit in range(4):
                tiles = rotate(tiles, bit, first[bit])
            for j in range(16):
                z = j >> 1
                p_buf[j & 1, z & 1, z >> 1, bw] = tiles[j]

    pl.semaphore_wait(barrier, 38)

    def send_z(source, target, c, g, send_sem, recv_sem):
        def one(h, p):
            pltpu.make_async_remote_copy(
                src_ref=source.at[c, p, h], dst_ref=target.at[c, my_p, my_h],
                send_sem=send_sem.at[c, g], recv_sem=recv_sem.at[c, g],
                device_id=z_device(2 * h + p), device_id_type=MESH,
            ).start()

        if g == 0:
            @pl.loop(0, 4)
            def _(k):
                one(lax.rem(my_h + k, 4), 1 - my_p)
        else:
            @pl.loop(1, 4)
            def _(k):
                one(lax.rem(my_h + k, 4), my_p)

    def wait_z(buffer, c, g, sem):
        part = buffer.at[c, 1 - my_p] if g == 0 else buffer.at[c, my_p, pl.ds(0, 3)]
        pltpu.make_async_copy(part, part, sem.at[c, g]).wait()

    def send_w(source, target, c, g, send_sem, recv_sem):
        p = 1 - my_p if g == 0 else my_p

        @pl.loop(1, 32)
        def _(k):
            w = other_w(k)
            pltpu.make_async_remote_copy(
                src_ref=source.at[c, p, :, w], dst_ref=target.at[c, p, :, my_w],
                send_sem=send_sem.at[c, g], recv_sem=recv_sem.at[c, g],
                device_id=w_device(w), device_id_type=MESH,
            ).start()

        for h in range(4):
            target[c, p, h, my_w] = source[c, p, h, my_w]

    def wait_w(buffer, c, g, sem):
        part = buffer.at[c, 0, :, pl.ds(0, 31)]
        pltpu.make_async_copy(part, part, sem.at[c, g]).wait()

    def rotate_bw(buffer, c, g, layer):
        gates = [gate(layer, q) for q in BW_QUBITS]
        p = 1 - my_p if g == 0 else my_p

        @pl.loop(0, 4)
        def _(h):
            tiles = [buffer[c, p, h, w] for w in range(32)]
            for bit in range(5):
                tiles = rotate(tiles, bit, gates[bit])
            for w in range(32):
                buffer[c, p, h, w] = tiles[w]

    for g in range(2):
        send_z(p_buf, q_buf, 0, g, fz_s, fz_r)
    q_buf[0, my_p, my_h] = p_buf[0, my_p, my_h]
    for g in range(2):
        rotate_bw(p_buf, 1, g, 0)
        send_w(p_buf, q_buf, 1, g, fw_s, fw_r)

    square = (256, 256)
    rows = lax.broadcasted_iota(jnp.int32, square, 0)
    cols = lax.broadcasted_iota(jnp.int32, square, 1)
    for layer in range(2):
        for side, qubits in enumerate((ROW_QUBITS, COL_QUBITS)):
            matrix = None
            for j, q in enumerate(qubits):
                cosine, sine = gate(layer, q, square)
                to, of = (rows, cols) if side == 0 else (cols, rows)
                a, b = to >> j & 1, of >> j & 1
                entry = jnp.where(a == b, cosine, jnp.where(a == 1, sine, -sine))
                matrix = entry if matrix is None else matrix * entry
            high, low = split(matrix)
            if side == 0:
                gate_left[layer, :256], gate_left[layer, 256:] = high, low
            else:
                gate_right[layer, 0], gate_right[layer, 1] = high, low

    w_row, p_col = rows >> 3, cols >> 7
    fixed = ladder(my_w, 5) + ladder(my_z, 3) + (my_w >> 4 & my_z & 1)
    cross = (
        ladder(cols & 127, 7) + (cols >> 6 & rows & 1) + ladder(rows & 7, 3) + (my_z >> 2 & w_row & 1)
        + (w_row & p_col & 1) + ladder(w_row >> 1, 4) + fixed
    )
    for h in range(4):
        with_h = cross + (p_col & h & 1) + (h >> 1 & w_row >> 1 & 1) + (h & h >> 1 & 1)
        cz[0, h] = signs(with_h)
        cz[1, h] = signs(with_h + (rows >> 2 & 1) + (my_w & 1))

    h_gates = [[gate(layer, q, (32, 256)) for q in (21, 22)] for layer in range(2)]

    def middle(c):
        def left(layer, block):
            high, low = split(block)
            both = jnp.dot(gate_left[layer], high, preferred_element_type=F32)
            return both[:256] + both[256:] + jnp.dot(gate_left[layer, :256], low, preferred_element_type=F32)

        def right(layer, block):
            high, low = split(block)
            both = jnp.dot(jnp.concatenate([high, low], axis=0), gate_right[layer, 0], preferred_element_type=F32)
            return both[:256] + both[256:] + jnp.dot(high, gate_right[layer, 1], preferred_element_type=F32)

        for h in range(4):
            block = jnp.concatenate([w_buf[c, p, h].reshape(256, 128) for p in range(2)], axis=1)
            ys[h] = right(0, left(0, block))

        @pl.loop(0, 8)
        def _(r):
            part = pl.ds(pl.multiple_of(32 * r, 32), 32)
            tiles = [ys[h, part] for h in range(4)]
            for layer in range(2):
                for bit in range(2):
                    tiles = rotate(tiles, bit, h_gates[layer][bit])
                if layer == 0:
                    tiles = [tiles[h] * cz[c, h, part] for h in range(4)]
            for h in range(4):
                ys[h, part] = tiles[h]

        for h in range(4):
            block = right(1, left(1, ys[h]))
            for p in range(2):
                m_buf[c, p, h] = block[:, 128 * p:128 * p + 128].reshape(32, 8, 128)

    def back(c, g):
        wait_w(v_buf, c, g, bw_r)
        rotate_bw(v_buf, c, g, 1)
        if c == 0 or g == 0:
            send_z(v_buf, t_buf, c, g, bz_s, bz_r)
        else:
            for i in range(QUARTERS):
                part = pl.ds(8 * i, 8)

                @pl.loop(1, 4)
                def _(k):
                    h = lax.rem(my_h + k, 4)
                    pltpu.make_async_remote_copy(
                        src_ref=v_buf.at[c, my_p, h, part], dst_ref=t_buf.at[c, my_p, my_h, part],
                        send_sem=last_s.at[i], recv_sem=last_r.at[i],
                        device_id=z_device(2 * h + my_p), device_id_type=MESH,
                    ).start()
        if g == 1:
            t_buf[c, my_p, my_h] = v_buf[c, my_p, my_h]

    wait_z(q_buf, 0, 0, fz_r)
    rotate_bw(q_buf, 0, 0, 0)
    send_w(q_buf, w_buf, 0, 0, fw_s, fw_r)
    wait_w(q_buf, 1, 0, fw_r)
    send_z(q_buf, w_buf, 1, 0, fz_s, fz_r)
    wait_z(q_buf, 0, 1, fz_r)
    rotate_bw(q_buf, 0, 1, 0)
    send_w(q_buf, w_buf, 0, 1, fw_s, fw_r)
    wait_w(q_buf, 1, 1, fw_r)
    send_z(q_buf, w_buf, 1, 1, fz_s, fz_r)
    w_buf[1, my_p, my_h] = q_buf[1, my_p, my_h]
    for g in range(2):
        wait_w(w_buf, 0, g, fw_r)
    middle(0)
    for g in range(2):
        send_w(m_buf, v_buf, 0, g, bw_s, bw_r)
    back(0, 0)
    for g in range(2):
        wait_z(w_buf, 1, g, fz_r)
    middle(1)
    for g in range(2):
        send_w(m_buf, v_buf, 1, g, bw_s, bw_r)
    back(0, 1)
    back(1, 0)
    back(1, 1)

    second = [gate(1, q) for q in (10, 16, 17, 18)]
    sub = lax.broadcasted_iota(jnp.int32, (8, 128), 0)
    lane = lax.broadcasted_iota(jnp.int32, (8, 128), 1)
    base = ladder(lane, 7) + (lane >> 6 & sub & 1) + ladder(sub, 3)
    base = base + ladder(dev, 5) + ladder(grp, 3) + (dev >> 4 & grp & 1)
    tile_signs = [signs(base + c * (sub >> 2 & 1)) for c in range(2)]
    for c, g in ((0, 0), (0, 1), (1, 0)):
        wait_z(t_buf, c, g, bz_r)
    for i in range(QUARTERS):
        part = t_buf.at[1, 0, pl.ds(0, 3), pl.ds(8 * i, 8)]
        pltpu.make_async_copy(part, part, last_r.at[i]).wait()

        @pl.loop(8 * i, 8 * i + 8)
        def _(bw):
            tiles = [t_buf[j & 1, j >> 1 & 1, j >> 2, bw] for j in range(16)]
            for bit in range(4):
                tiles = rotate(tiles, bit, second[bit])
            for j in range(16):
                c, z = j & 1, j >> 1
                parity = ladder(bw, 5) + (c & bw & 1) + (bw >> 4 & z & 1) + (z >> 2 & core & 1)
                parity = parity + (z & z >> 1 & 1) + (z >> 1 & z >> 2 & 1)
                out[z, bw, c] = tiles[j] * (tile_signs[c] * signs(parity))

    for c in range(2):
        for g in range(2):
            wait_z(p_buf, c, g, fz_s)
            wait_w(q_buf, c, g, fw_s)
            wait_w(m_buf, c, g, bw_s)
            if c == 0 or g == 0:
                wait_z(v_buf, c, g, bz_s)
    for i in range(QUARTERS):
        part = v_buf.at[1, 0, pl.ds(0, 3), pl.ds(8 * i, 8)]
        pltpu.make_async_copy(part, part, last_s.at[i]).wait()


def shards(state, angles):
    view = (8, 32, 2, 8, 128)
    by_z = (2, 2, 4, 32, 8, 128)
    pairs = pltpu.SemaphoreType.DMA((2, 2))
    quarters = pltpu.SemaphoreType.DMA((QUARTERS,))
    out = pl.pallas_call(
        kernel,
        out_shape=jax.ShapeDtypeStruct(view, F32),
        in_specs=[pl.BlockSpec(memory_space=pltpu.HBM)] * 2,
        out_specs=pl.BlockSpec(memory_space=pltpu.VMEM),
        scratch_shapes=[
            pltpu.VMEM(view, F32), pltpu.VMEM((2, 27), F32),
            pltpu.VMEM(by_z, F32), pltpu.VMEM(by_z, F32), pltpu.VMEM(by_z, F32),
            pltpu.VMEM(by_z, F32), pltpu.VMEM(by_z, F32), pltpu.VMEM(by_z, F32),
            pltpu.VMEM((4, 256, 256), F32),
            pltpu.VMEM((2, 4, 256, 256), F32),
            pltpu.VMEM((2, 512, 256), BF16), pltpu.VMEM((2, 2, 256, 256), BF16),
            quarters, pltpu.SemaphoreType.DMA,
            pairs, pairs, pairs, pairs, pairs, pairs, pairs, pairs,
            quarters, quarters,
        ],
        compiler_params=pltpu.CompilerParams(
            collective_id=0, has_side_effects=True, vmem_limit_bytes=50 * 2**20
        ),
    )(state.reshape(view), angles)
    return out.reshape(state.shape)


def solution(mesh):
    placed = (P("grp", "dev", None), P())
    return jax.shard_map(
        shards, mesh=mesh, in_specs=placed, out_specs=P("grp", "dev", None), check_vma=False
    )
```

```python
import jax
import jax.numpy as jnp
from jax import lax
from jax.experimental import pallas as pl
from jax.experimental.pallas import tpu as pltpu
from jax.sharding import PartitionSpec as P

MESH = pl.DeviceIdType.MESH
F32, BF16 = jnp.float32, jnp.bfloat16
W_QUBITS = (19, 23, 24, 25, 26)
BW_QUBITS = (11, 12, 13, 14, 15)
ROW_QUBITS = (7, 8, 9) + W_QUBITS
COL_QUBITS = (0, 1, 2, 3, 4, 5, 6, 20)
QUARTERS = 4


def rotate(tiles, bit, gate):
    cosine, sine = gate
    out = list(tiles)
    for i in range(len(tiles)):
        if not i >> bit & 1:
            j = i | 1 << bit
            out[i] = cosine * tiles[i] - sine * tiles[j]
            out[j] = sine * tiles[i] + cosine * tiles[j]
    return out


def ladder(values, nbits):
    total = values & values >> 1
    parity = total & 1
    for j in range(1, nbits - 1):
        parity = parity + (total >> j & 1)
    return parity


def signs(parity):
    return (1 - 2 * (parity & 1)).astype(F32)


def split(value):
    high = value.astype(BF16)
    return high, (value - high.astype(F32)).astype(BF16)


def dot3(a, b):
    return (
        jnp.dot(a[0], b[0], preferred_element_type=F32)
        + jnp.dot(a[0], b[1], preferred_element_type=F32)
        + jnp.dot(a[1], b[0], preferred_element_type=F32)
    )


def at_w(w):
    return lax.div(w, 16), lax.rem(lax.div(w, 4), 4), lax.rem(lax.div(w, 2), 2), lax.rem(w, 2)


def kernel(
    state, angles, out,
    x, turns, p_buf, q_buf, w_buf, m_buf, v_buf, t_buf, r_buf, fx_buf, fy_buf, bx_buf, by_buf, ys, cz,
    gate_left, gate_right, gate_lane,
    load_sem, turns_sem, z_s, z_r, half_s, half_r, last_s, last_r, fx_s, fx_r, fy_s, fy_r, fc_s, fc_r, bx_s, bx_r, by_s, by_r, bc_s, bc_r,
):
    grp, dev = lax.axis_index("grp"), lax.axis_index("dev")
    core, my_z, x_lo = lax.rem(dev, 2), lax.rem(lax.div(dev, 2), 8), lax.div(dev, 16)
    my_y, x_hi = lax.rem(grp, 4), lax.div(grp, 4)
    my_w = core + 2 * x_lo + 4 * grp
    my_p, my_h = lax.rem(my_z, 2), lax.div(my_z, 2)

    def z_device(z):
        return (grp, 16 * x_lo + 2 * z + core)

    def x_peer(k):
        there = lax.rem(2 * x_hi + x_lo + k, 4)
        return lax.div(there, 2), lax.rem(there, 2)

    def x_device(hi, lo):
        return (4 * hi + my_y, 16 * lo + 2 * my_z + core)

    def y_device(y):
        return (4 * x_hi + y, dev)

    core_device = (grp, dev + 1 - 2 * core)

    def load(i):
        part = pl.ds(8 * i, 8)
        return pltpu.make_async_copy(state.at[:, part], x.at[:, part], load_sem.at[i])

    load_turns = pltpu.make_async_copy(angles, turns, turns_sem)
    load_turns.start()
    for i in range(QUARTERS):
        load(i).start()
    barrier = pltpu.get_barrier_semaphore()

    @pl.loop(1, 8)
    def _(k):
        pl.semaphore_signal(barrier, inc=1, device_id=z_device(lax.rem(my_z + k, 8)), device_id_type=MESH)

    @pl.loop(1, 4)
    def _(k):
        pl.semaphore_signal(barrier, inc=1, device_id=x_device(*x_peer(k)), device_id_type=MESH)
        pl.semaphore_signal(barrier, inc=1, device_id=y_device(lax.rem(my_y + k, 4)), device_id_type=MESH)

    pl.semaphore_signal(barrier, inc=1, device_id=core_device, device_id_type=MESH)

    load_turns.wait()
    half = 0.5 * turns[...]
    cosines, sines = jnp.cos(half), jnp.sin(half)

    def gate(layer, qubit, shape=(8, 128)):
        at = (slice(layer, layer + 1), slice(qubit, qubit + 1))
        return jnp.broadcast_to(cosines[at], shape), jnp.broadcast_to(sines[at], shape)

    first = [gate(0, q) for q in (10, 16, 17, 18)]
    for i in range(QUARTERS):
        load(i).wait()

        @pl.loop(8 * i, 8 * i + 8)
        def _(bw):
            tiles = [x[j >> 1, bw, j & 1] for j in range(16)]
            place = at_w(bw)
            for bit in range(4):
                tiles = rotate(tiles, bit, first[bit])
            for j in range(16):
                z = j >> 1
                p_buf[(j & 1, z & 1, z >> 1) + place] = tiles[j]

    pl.semaphore_wait(barrier, 14)

    def parity(g):
        return 1 - my_p if g == 0 else my_p

    def to_z(source, target, place, h, p, send_sem, recv_sem):
        pltpu.make_async_remote_copy(
            src_ref=source.at[(place[0], p, h) + place[1:]], dst_ref=target.at[(place[0], my_p, my_h) + place[1:]],
            send_sem=send_sem, recv_sem=recv_sem, device_id=z_device(2 * h + p), device_id_type=MESH,
        ).start()

    def send_z(source, target, place, g, send_sem, recv_sem):
        if g == 0:
            @pl.loop(0, 4)
            def _(h):
                to_z(source, target, place, h, 1 - my_p, send_sem, recv_sem)
        else:
            @pl.loop(0, 3)
            def _(k):
                to_z(source, target, place, k + lax.div(k + 4 - my_h, 4), my_p, send_sem, recv_sem)

    def wait_z(buffer, place, g, sem):
        part = buffer.at[(place[0], 0, pl.ds(0, 4 - g)) + place[1:]]
        pltpu.make_async_copy(part, part, sem).wait()

    def send_x(source, target, c, g, send_sem, recv_sem):
        p = parity(g)

        @pl.loop(1, 4)
        def _(k):
            hi, lo = x_peer(k)
            pltpu.make_async_remote_copy(
                src_ref=source.at[c, p, :, hi, :, lo], dst_ref=target.at[c, p, :, x_hi, :, x_lo],
                send_sem=send_sem.at[c, g], recv_sem=recv_sem.at[c, g],
                device_id=x_device(hi, lo), device_id_type=MESH,
            ).start()

        target[c, p, :, x_hi, :, x_lo] = source[c, p, :, x_hi, :, x_lo]

    def send_y(source, target, c, g, send_sem, recv_sem):
        p = parity(g)

        @pl.loop(1, 4)
        def _(k):
            y = lax.rem(my_y + k, 4)
            pltpu.make_async_remote_copy(
                src_ref=source.at[c, p, :, :, y], dst_ref=target.at[c, p, :, :, my_y],
                send_sem=send_sem.at[c, g], recv_sem=recv_sem.at[c, g],
                device_id=y_device(y), device_id_type=MESH,
            ).start()

        target[c, p, :, :, my_y] = source[c, p, :, :, my_y]

    def send_core(source, target, c, g, send_sem, recv_sem):
        p = parity(g)
        pltpu.make_async_remote_copy(
            src_ref=source.at[c, p, :, :, :, :, 1 - core], dst_ref=target.at[c, p, :, :, :, :, core],
            send_sem=send_sem.at[c, g], recv_sem=recv_sem.at[c, g],
            device_id=core_device, device_id_type=MESH,
        ).start()
        target[c, p, :, :, :, :, core] = source[c, p, :, :, :, :, core]

    def wait_w(c, g, sem, n=3):
        part = t_buf.at[0, 0, pl.ds(0, n)]
        pltpu.make_async_copy(part, part, sem.at[c, g]).wait()

    def hop(n, source, target, c, g, sems):
        if (n + g) % 2 == 0:
            send_x(source, target, c, g, sems[0], sems[1])
        else:
            send_y(source, target, c, g, sems[2], sems[3])

    def wait_hop(n, c, g, sems):
        wait_w(c, g, sems[1] if (n + g) % 2 == 0 else sems[3])

    forth, home = (fx_s, fx_r, fy_s, fy_r), (bx_s, bx_r, by_s, by_r)

    def rotate_bw(buffer, c, g, layer):
        gates = [gate(layer, q) for q in BW_QUBITS]
        p = parity(g)

        @pl.loop(0, 4)
        def _(h):
            spots = [(c, p, h, w >> 4, w >> 2 & 3, w >> 1 & 1, w & 1) for w in range(32)]
            tiles = [buffer[spot] for spot in spots]
            for bit in range(5):
                tiles = rotate(tiles, bit, gates[bit])
            for spot, tile in zip(spots, tiles):
                buffer[spot] = tile

    for g in range(2):
        send_z(p_buf, q_buf, (0,), g, z_s.at[g], z_r.at[g])
    for g in range(2):
        rotate_bw(p_buf, 1, g, 0)
        hop(0, p_buf, fx_buf, 1, g, forth)
    q_buf[0, my_p, my_h] = p_buf[0, my_p, my_h]

    square = (256, 256)
    rows = lax.broadcasted_iota(jnp.int32, square, 0)
    cols = lax.broadcasted_iota(jnp.int32, square, 1)
    for layer in range(2):
        for side, qubits in enumerate((ROW_QUBITS, COL_QUBITS)):
            matrix = None
            for j, q in enumerate(qubits):
                cosine, sine = gate(layer, q, square)
                to, of = (rows, cols) if side == 0 else (cols, rows)
                a, b = to >> j & 1, of >> j & 1
                entry = jnp.where(a == b, cosine, jnp.where(a == 1, sine, -sine))
                lanes = jnp.where(a == b, matrix, 0.0) if j == 7 else None
                matrix = entry if matrix is None else matrix * entry
            high, low = split(matrix)
            if side == 0:
                gate_left[layer, :256], gate_left[layer, 256:] = high, low
            else:
                gate_right[layer, 0], gate_right[layer, 1] = high, low
                gate_lane[layer, 0], gate_lane[layer, 1] = split(lanes)

    w_row, p_col = rows >> 3, cols >> 7
    fixed = ladder(my_w, 5) + ladder(my_z, 3) + (my_w >> 4 & my_z & 1)
    cross = (
        ladder(cols & 127, 7) + (cols >> 6 & rows & 1) + ladder(rows & 7, 3) + (my_z >> 2 & w_row & 1)
        + (w_row & p_col & 1) + ladder(w_row >> 1, 4) + fixed
    )
    for h in range(4):
        with_h = cross + (p_col & h & 1) + (h >> 1 & w_row >> 1 & 1) + (h & h >> 1 & 1)
        cz[0, h] = signs(with_h)
        cz[1, h] = signs(with_h + (rows >> 2 & 1) + (my_w & 1))

    h_gates = [[gate(layer, q, (32, 256)) for q in (21, 22)] for layer in range(2)]

    def left(layer, block):
        high, low = split(block)
        both = jnp.dot(gate_left[layer], high, preferred_element_type=F32)
        return both[:256] + both[256:] + jnp.dot(gate_left[layer, :256], low, preferred_element_type=F32)

    def right(gates, layer, block):
        high, low = split(block)
        both = jnp.dot(jnp.concatenate([high, low], axis=0), gates[layer, 0], preferred_element_type=F32)
        return both[:256] + both[256:] + jnp.dot(high, gates[layer, 1], preferred_element_type=F32)

    def rows_and_lanes(buffer, g, layer):
        p = parity(g)
        for h in (0, 2):
            block = jnp.concatenate([buffer[1, p, h + i].reshape(256, 128) for i in range(2)], axis=1)
            block = right(gate_lane, layer, left(layer, block))
            for i in range(2):
                buffer[1, p, h + i] = block[:, 128 * i:128 * i + 128].reshape(2, 4, 2, 2, 8, 128)

    z_gates = [[gate(layer, q) for q in (20, 21, 22)] for layer in range(2)]

    def middle_z(half):
        @pl.loop(0, 16)
        def _(k):
            w = 16 * half + k
            place = at_w(w)
            tiles = [w_buf[(1, z & 1, z >> 1) + place] for z in range(8)]
            for bit in range(3):
                tiles = rotate(tiles, bit, z_gates[0][bit])
            part = pl.ds(pl.multiple_of(8 * w, 8), 8)
            for z in range(8):
                tiles[z] = tiles[z] * cz[1, z >> 1, part, 128 * (z & 1):128 * (z & 1) + 128]
            for bit in range(3):
                tiles = rotate(tiles, bit, z_gates[1][bit])
            for z in range(8):
                m_buf[(1, z & 1, z >> 1) + place] = tiles[z]

    def middle(c):
        for h in range(4):
            block = jnp.concatenate([w_buf[c, p, h].reshape(256, 128) for p in range(2)], axis=1)
            ys[h] = right(gate_right, 0, left(0, block))

        @pl.loop(0, 8)
        def _(r):
            part = pl.ds(pl.multiple_of(32 * r, 32), 32)
            tiles = [ys[h, part] for h in range(4)]
            for layer in range(2):
                for bit in range(2):
                    tiles = rotate(tiles, bit, h_gates[layer][bit])
                if layer == 0:
                    tiles = [tiles[h] * cz[c, h, part] for h in range(4)]
            for h in range(4):
                ys[h, part] = tiles[h]

        for h in range(4):
            block = right(gate_right, 1, left(1, ys[h]))
            for p in range(2):
                m_buf[c, p, h] = block[:, 128 * p:128 * p + 128].reshape(2, 4, 2, 2, 8, 128)

    def forward_1(g):
        wait_w(1, g, fc_r, 2)
        rows_and_lanes(q_buf, g, 0)

    def back_0(g):
        wait_w(0, g, bc_r, 2)
        rotate_bw(v_buf, 0, g, 1)
        if g == 0:
            send_z(v_buf, t_buf, (0,), 0, z_s.at[2], z_r.at[2])
            return

        @pl.loop(0, 3)
        def _(k):
            h = k + lax.div(k + 4 - my_h, 4)
            for i in range(QUARTERS):
                to_z(v_buf, t_buf, (0, i >> 1, pl.ds(2 * (i & 1), 2)), h, my_p, last_s.at[i], last_r.at[i])

        t_buf[0, my_p, my_h] = v_buf[0, my_p, my_h]

    for g in range(2):
        wait_hop(0, 1, g, forth)
        hop(1, fx_buf, fy_buf, 1, g, forth)
    for g in range(2):
        wait_hop(1, 1, g, forth)
        send_core(fy_buf, q_buf, 1, g, fc_s, fc_r)
    for g in range(2):
        forward_1(g)
    for half in range(2):
        for g in range(2):
            send_z(q_buf, w_buf, (1, half), g, half_s.at[0, half, g], half_r.at[0, half, g])
    w_buf[1, my_p, my_h] = q_buf[1, my_p, my_h]
    for g in range(2):
        wait_z(q_buf, (0,), g, z_r.at[g])
        rotate_bw(q_buf, 0, g, 0)
        hop(0, q_buf, fx_buf, 0, g, forth)
    for g in range(2):
        wait_hop(0, 0, g, forth)
        hop(1, fx_buf, fy_buf, 0, g, forth)

    def turn_1(half):
        for g in range(2):
            wait_z(w_buf, (1, half), g, half_r.at[0, half, g])
        middle_z(half)
        for g in range(2):
            send_z(m_buf, r_buf, (1, half), g, half_s.at[1, half, g], half_r.at[1, half, g])

    turn_1(0)
    for g in range(2):
        wait_hop(1, 0, g, forth)
        send_core(fy_buf, w_buf, 0, g, fc_s, fc_r)
    for g in range(2):
        wait_w(0, g, fc_r, 2)
    middle(0)
    for g in range(2):
        hop(0, m_buf, bx_buf, 0, g, home)
    turn_1(1)
    r_buf[1, my_p, my_h] = m_buf[1, my_p, my_h]
    for g in range(2):
        wait_hop(0, 0, g, home)
        hop(1, bx_buf, by_buf, 0, g, home)
    for g in range(2):
        wait_hop(1, 0, g, home)
        send_core(by_buf, v_buf, 0, g, bc_s, bc_r)
    for g in range(2):
        back_0(g)
    for half in range(2):
        for g in range(2):
            wait_z(r_buf, (1, half), g, half_r.at[1, half, g])
    for g in range(2):
        rows_and_lanes(r_buf, g, 1)
        hop(0, r_buf, bx_buf, 1, g, home)
    for g in range(2):
        wait_hop(0, 1, g, home)
        hop(1, bx_buf, by_buf, 1, g, home)
    for g in range(2):
        wait_hop(1, 1, g, home)
        send_core(by_buf, t_buf, 1, g, bc_s, bc_r)
    for g in range(2):
        wait_w(1, g, bc_r, 2)
        rotate_bw(t_buf, 1, g, 1)

    second = [gate(1, q) for q in (10, 16, 17, 18)]
    sub = lax.broadcasted_iota(jnp.int32, (8, 128), 0)
    lane = lax.broadcasted_iota(jnp.int32, (8, 128), 1)
    base = ladder(lane, 7) + (lane >> 6 & sub & 1) + ladder(sub, 3)
    base = base + ladder(dev, 5) + ladder(grp, 3) + (dev >> 4 & grp & 1)
    tile_signs = [signs(base + c * (sub >> 2 & 1)) for c in range(2)]
    wait_z(t_buf, (0,), 0, z_r.at[2])
    for i in range(QUARTERS):
        wait_z(t_buf, (0, i >> 1, pl.ds(2 * (i & 1), 2)), 1, last_r.at[i])

        @pl.loop(8 * i, 8 * i + 8)
        def _(bw):
            place = at_w(bw)
            tiles = [t_buf[(j & 1, j >> 1 & 1, j >> 2) + place] for j in range(16)]
            for bit in range(4):
                tiles = rotate(tiles, bit, second[bit])
            for j in range(16):
                c, z = j & 1, j >> 1
                odd = ladder(bw, 5) + (c & bw & 1) + (bw >> 4 & z & 1) + (z >> 2 & core & 1)
                odd = odd + (z & z >> 1 & 1) + (z >> 1 & z >> 2 & 1)
                out[z, bw, c] = tiles[j] * (tile_signs[c] * signs(odd))

    for g in range(2):
        wait_z(p_buf, (0,), g, z_s.at[g])
        for half in range(2):
            for way in range(2):
                wait_z(r_buf, (1, half), g, half_s.at[way, half, g])
        for c in range(2):
            for sem, n in ((fx_s, 3), (fy_s, 3), (fc_s, 2), (bx_s, 3), (by_s, 3), (bc_s, 2)):
                wait_w(c, g, sem, n)
    wait_z(v_buf, (0,), 0, z_s.at[2])
    for i in range(QUARTERS):
        wait_z(v_buf, (0, i >> 1, pl.ds(2 * (i & 1), 2)), 1, last_s.at[i])


def shards(state, angles):
    view = (8, 32, 2, 8, 128)
    by_z = (2, 2, 4, 2, 4, 2, 2, 8, 128)
    pairs = pltpu.SemaphoreType.DMA((2, 2))
    quarters = pltpu.SemaphoreType.DMA((QUARTERS,))
    out = pl.pallas_call(
        kernel,
        out_shape=jax.ShapeDtypeStruct(view, F32),
        in_specs=[pl.BlockSpec(memory_space=pltpu.HBM)] * 2,
        out_specs=pl.BlockSpec(memory_space=pltpu.VMEM),
        scratch_shapes=[
            pltpu.VMEM(view, F32), pltpu.VMEM((2, 27), F32),
            *[pltpu.VMEM(by_z, F32)] * 11,
            pltpu.VMEM((4, 256, 256), F32),
            pltpu.VMEM((2, 4, 256, 256), F32),
            pltpu.VMEM((2, 512, 256), BF16), pltpu.VMEM((2, 2, 256, 256), BF16), pltpu.VMEM((2, 2, 256, 256), BF16),
            quarters, pltpu.SemaphoreType.DMA,
            pltpu.SemaphoreType.DMA((3,)), pltpu.SemaphoreType.DMA((3,)),
            pltpu.SemaphoreType.DMA((2, 2, 2)), pltpu.SemaphoreType.DMA((2, 2, 2)),
            quarters, quarters,
            *[pairs] * 12,
        ],
        compiler_params=pltpu.CompilerParams(
            collective_id=0, has_side_effects=True, vmem_limit_bytes=50 * 2**20
        ),
    )(state.reshape(view), angles)
    return out.reshape(state.shape)


def solution(mesh):
    placed = (P("grp", "dev", None), P())
    return jax.shard_map(
        shards, mesh=mesh, in_specs=placed, out_specs=P("grp", "dev", None), check_vma=False
    )
```

```python
import jax
import jax.numpy as jnp
from jax import lax
from jax.experimental import pallas as pl
from jax.experimental.pallas import tpu as pltpu
from jax.sharding import PartitionSpec as P

MESH = pl.DeviceIdType.MESH
F32, BF16 = jnp.float32, jnp.bfloat16
W_QUBITS = (19, 23, 24, 25, 26)
BW_QUBITS = (11, 12, 13, 14, 15)
ROW_QUBITS = (7, 8, 9) + W_QUBITS
COL_QUBITS = (0, 1, 2, 3, 4, 5, 6, 20)
QUARTERS = 4


def rotate(tiles, bit, gate):
    cosine, sine = gate
    out = list(tiles)
    for i in range(len(tiles)):
        if not i >> bit & 1:
            j = i | 1 << bit
            out[i] = cosine * tiles[i] - sine * tiles[j]
            out[j] = sine * tiles[i] + cosine * tiles[j]
    return out


def ladder(values, nbits):
    total = values & values >> 1
    parity = total & 1
    for j in range(1, nbits - 1):
        parity = parity + (total >> j & 1)
    return parity


def signs(parity):
    return (1 - 2 * (parity & 1)).astype(F32)


def split(value):
    high = value.astype(BF16)
    return high, (value - high.astype(F32)).astype(BF16)


def dot3(a, b):
    return (
        jnp.dot(a[0], b[0], preferred_element_type=F32)
        + jnp.dot(a[0], b[1], preferred_element_type=F32)
        + jnp.dot(a[1], b[0], preferred_element_type=F32)
    )


def at_w(w):
    return lax.div(w, 16), lax.rem(lax.div(w, 4), 4), lax.rem(lax.div(w, 2), 2), lax.rem(w, 2)


def kernel(
    state, angles, out,
    x, turns, p_buf, q_buf, w_buf, m_buf, v_buf, t_buf, r_buf, fx_buf, fy_buf, bx_buf, by_buf, ys, cz,
    gate_left, gate_right, gate_lane,
    load_sem, turns_sem, z_s, z_r, half_s, half_r, last_s, last_r, fx_s, fx_r, fy_s, fy_r, fc_s, fc_r, bx_s, bx_r, by_s, by_r, bc_s, bc_r,
):
    grp, dev = lax.axis_index("grp"), lax.axis_index("dev")
    core, my_z, x_lo = lax.rem(dev, 2), lax.rem(lax.div(dev, 2), 8), lax.div(dev, 16)
    my_y, x_hi = lax.rem(grp, 4), lax.div(grp, 4)
    my_w = core + 2 * x_lo + 4 * grp
    my_p, my_h = lax.rem(my_z, 2), lax.div(my_z, 2)

    def z_device(z):
        return (grp, 16 * x_lo + 2 * z + core)

    def x_peer(k):
        there = lax.rem(2 * x_hi + x_lo + k, 4)
        return lax.div(there, 2), lax.rem(there, 2)

    def x_device(hi, lo):
        return (4 * hi + my_y, 16 * lo + 2 * my_z + core)

    def y_device(y):
        return (4 * x_hi + y, dev)

    core_device = (grp, dev + 1 - 2 * core)

    def load(i):
        part = pl.ds(8 * i, 8)
        return pltpu.make_async_copy(state.at[:, part], x.at[:, part], load_sem.at[i])

    load_turns = pltpu.make_async_copy(angles, turns, turns_sem)
    load_turns.start()
    for i in range(QUARTERS):
        load(i).start()
    barrier = pltpu.get_barrier_semaphore()

    @pl.loop(1, 8)
    def _(k):
        pl.semaphore_signal(barrier, inc=1, device_id=z_device(lax.rem(my_z + k, 8)), device_id_type=MESH)

    @pl.loop(1, 4)
    def _(k):
        pl.semaphore_signal(barrier, inc=1, device_id=x_device(*x_peer(k)), device_id_type=MESH)
        pl.semaphore_signal(barrier, inc=1, device_id=y_device(lax.rem(my_y + k, 4)), device_id_type=MESH)

    pl.semaphore_signal(barrier, inc=1, device_id=core_device, device_id_type=MESH)

    load_turns.wait()
    half = 0.5 * turns[...]
    cosines, sines = jnp.cos(half), jnp.sin(half)

    def gate(layer, qubit, shape=(8, 128)):
        at = (slice(layer, layer + 1), slice(qubit, qubit + 1))
        return jnp.broadcast_to(cosines[at], shape), jnp.broadcast_to(sines[at], shape)

    first = [gate(0, q) for q in (10, 16, 17, 18)]
    def quarter(i):
        return i >> 1, pl.ds(2 * (i & 1), 2)

    def parity(g):
        return 1 - my_p if g == 0 else my_p

    def to_z(source, target, place, h, p, send_sem, recv_sem):
        pltpu.make_async_remote_copy(
            src_ref=source.at[(place[0], p, h) + place[1:]], dst_ref=target.at[(place[0], my_p, my_h) + place[1:]],
            send_sem=send_sem, recv_sem=recv_sem, device_id=z_device(2 * h + p), device_id_type=MESH,
        ).start()

    def send_z(source, target, place, g, send_sem, recv_sem):
        if g == 0:
            @pl.loop(0, 4)
            def _(h):
                to_z(source, target, place, h, 1 - my_p, send_sem, recv_sem)
        else:
            @pl.loop(0, 3)
            def _(k):
                to_z(source, target, place, k + lax.div(k + 4 - my_h, 4), my_p, send_sem, recv_sem)

    def wait_z(buffer, place, g, sem):
        part = buffer.at[(place[0], 0, pl.ds(0, 4 - g)) + place[1:]]
        pltpu.make_async_copy(part, part, sem).wait()

    def send_x(source, target, c, g, send_sem, recv_sem):
        p = parity(g)

        @pl.loop(1, 4)
        def _(k):
            hi, lo = x_peer(k)
            pltpu.make_async_remote_copy(
                src_ref=source.at[c, p, :, hi, :, lo], dst_ref=target.at[c, p, :, x_hi, :, x_lo],
                send_sem=send_sem.at[c, g], recv_sem=recv_sem.at[c, g],
                device_id=x_device(hi, lo), device_id_type=MESH,
            ).start()

        target[c, p, :, x_hi, :, x_lo] = source[c, p, :, x_hi, :, x_lo]

    def send_y(source, target, c, g, send_sem, recv_sem):
        p = parity(g)

        @pl.loop(1, 4)
        def _(k):
            y = lax.rem(my_y + k, 4)
            pltpu.make_async_remote_copy(
                src_ref=source.at[c, p, :, :, y], dst_ref=target.at[c, p, :, :, my_y],
                send_sem=send_sem.at[c, g], recv_sem=recv_sem.at[c, g],
                device_id=y_device(y), device_id_type=MESH,
            ).start()

        target[c, p, :, :, my_y] = source[c, p, :, :, my_y]

    def send_core(source, target, c, g, send_sem, recv_sem):
        p = parity(g)
        pltpu.make_async_remote_copy(
            src_ref=source.at[c, p, :, :, :, :, 1 - core], dst_ref=target.at[c, p, :, :, :, :, core],
            send_sem=send_sem.at[c, g], recv_sem=recv_sem.at[c, g],
            device_id=core_device, device_id_type=MESH,
        ).start()
        target[c, p, :, :, :, :, core] = source[c, p, :, :, :, :, core]

    def wait_w(c, g, sem, n=3):
        part = t_buf.at[0, 0, pl.ds(0, n)]
        pltpu.make_async_copy(part, part, sem.at[c, g]).wait()

    def hop(n, source, target, c, g, sems):
        if (n + g) % 2 == 0:
            send_x(source, target, c, g, sems[0], sems[1])
        else:
            send_y(source, target, c, g, sems[2], sems[3])

    def wait_hop(n, c, g, sems):
        wait_w(c, g, sems[1] if (n + g) % 2 == 0 else sems[3])

    forth, home = (fx_s, fx_r, fy_s, fy_r), (bx_s, bx_r, by_s, by_r)

    def rotate_bw(buffer, c, g, layer):
        gates = [gate(layer, q) for q in BW_QUBITS]
        p = parity(g)

        @pl.loop(0, 4)
        def _(h):
            spots = [(c, p, h, w >> 4, w >> 2 & 3, w >> 1 & 1, w & 1) for w in range(32)]
            tiles = [buffer[spot] for spot in spots]
            for bit in range(5):
                tiles = rotate(tiles, bit, gates[bit])
            for spot, tile in zip(spots, tiles):
                buffer[spot] = tile

    for i in range(QUARTERS):
        load(i).wait()

        @pl.loop(8 * i, 8 * i + 8)
        def _(bw):
            tiles = [x[j >> 1, bw, j & 1] for j in range(16)]
            place = at_w(bw)
            for bit in range(4):
                tiles = rotate(tiles, bit, first[bit])
            for j in range(16):
                z = j >> 1
                p_buf[(j & 1, z & 1, z >> 1) + place] = tiles[j]

        if i == 0:
            pl.semaphore_wait(barrier, 14)
        for g in range(2):
            send_z(p_buf, q_buf, (0,) + quarter(i), g, z_s.at[g], z_r.at[g])

    for g in range(2):
        rotate_bw(p_buf, 1, g, 0)
        hop(0, p_buf, fx_buf, 1, g, forth)
    q_buf[0, my_p, my_h] = p_buf[0, my_p, my_h]

    square = (256, 256)
    rows = lax.broadcasted_iota(jnp.int32, square, 0)
    cols = lax.broadcasted_iota(jnp.int32, square, 1)
    for layer in range(2):
        for side, qubits in enumerate((ROW_QUBITS, COL_QUBITS)):
            matrix = None
            for j, q in enumerate(qubits):
                cosine, sine = gate(layer, q, square)
                to, of = (rows, cols) if side == 0 else (cols, rows)
                a, b = to >> j & 1, of >> j & 1
                entry = jnp.where(a == b, cosine, jnp.where(a == 1, sine, -sine))
                lanes = jnp.where(a == b, matrix, 0.0) if j == 7 else None
                matrix = entry if matrix is None else matrix * entry
            high, low = split(matrix)
            if side == 0:
                gate_left[layer, :256], gate_left[layer, 256:] = high, low
            else:
                gate_right[layer, 0], gate_right[layer, 1] = high, low
                gate_lane[layer, 0], gate_lane[layer, 1] = split(lanes)

    w_row, p_col = rows >> 3, cols >> 7
    fixed = ladder(my_w, 5) + ladder(my_z, 3) + (my_w >> 4 & my_z & 1)
    cross = (
        ladder(cols & 127, 7) + (cols >> 6 & rows & 1) + ladder(rows & 7, 3) + (my_z >> 2 & w_row & 1)
        + (w_row & p_col & 1) + ladder(w_row >> 1, 4) + fixed
    )
    for h in range(4):
        with_h = cross + (p_col & h & 1) + (h >> 1 & w_row >> 1 & 1) + (h & h >> 1 & 1)
        cz[0, h] = signs(with_h)
        cz[1, h] = signs(with_h + (rows >> 2 & 1) + (my_w & 1))

    h_gates = [[gate(layer, q, (32, 256)) for q in (21, 22)] for layer in range(2)]

    def left(layer, block):
        high, low = split(block)
        both = jnp.dot(gate_left[layer], high, preferred_element_type=F32)
        return both[:256] + both[256:] + jnp.dot(gate_left[layer, :256], low, preferred_element_type=F32)

    def right(gates, layer, block):
        high, low = split(block)
        both = jnp.dot(jnp.concatenate([high, low], axis=0), gates[layer, 0], preferred_element_type=F32)
        return both[:256] + both[256:] + jnp.dot(high, gates[layer, 1], preferred_element_type=F32)

    def rows_and_lanes(buffer, g, layer):
        p = parity(g)
        for h in (0, 2):
            block = jnp.concatenate([buffer[1, p, h + i].reshape(256, 128) for i in range(2)], axis=1)
            block = right(gate_lane, layer, left(layer, block))
            for i in range(2):
                buffer[1, p, h + i] = block[:, 128 * i:128 * i + 128].reshape(2, 4, 2, 2, 8, 128)

    z_gates = [[gate(layer, q) for q in (20, 21, 22)] for layer in range(2)]

    def middle_z(half):
        @pl.loop(0, 16)
        def _(k):
            w = 16 * half + k
            place = at_w(w)
            tiles = [w_buf[(1, z & 1, z >> 1) + place] for z in range(8)]
            for bit in range(3):
                tiles = rotate(tiles, bit, z_gates[0][bit])
            part = pl.ds(pl.multiple_of(8 * w, 8), 8)
            for z in range(8):
                tiles[z] = tiles[z] * cz[1, z >> 1, part, 128 * (z & 1):128 * (z & 1) + 128]
            for bit in range(3):
                tiles = rotate(tiles, bit, z_gates[1][bit])
            for z in range(8):
                m_buf[(1, z & 1, z >> 1) + place] = tiles[z]

    def middle(c):
        for h in range(4):
            block = jnp.concatenate([w_buf[c, p, h].reshape(256, 128) for p in range(2)], axis=1)
            ys[h] = right(gate_right, 0, left(0, block))

        @pl.loop(0, 8)
        def _(r):
            part = pl.ds(pl.multiple_of(32 * r, 32), 32)
            tiles = [ys[h, part] for h in range(4)]
            for layer in range(2):
                for bit in range(2):
                    tiles = rotate(tiles, bit, h_gates[layer][bit])
                if layer == 0:
                    tiles = [tiles[h] * cz[c, h, part] for h in range(4)]
            for h in range(4):
                ys[h, part] = tiles[h]

        for h in range(4):
            block = right(gate_right, 1, left(1, ys[h]))
            for p in range(2):
                m_buf[c, p, h] = block[:, 128 * p:128 * p + 128].reshape(2, 4, 2, 2, 8, 128)

    def forward_1(g):
        wait_w(1, g, fc_r, 2)
        rows_and_lanes(q_buf, g, 0)

    def back_0(g):
        wait_w(0, g, bc_r, 2)
        rotate_bw(v_buf, 0, g, 1)
        if g == 0:
            send_z(v_buf, t_buf, (0,), 0, z_s.at[2], z_r.at[2])
            return

        @pl.loop(0, 3)
        def _(k):
            h = k + lax.div(k + 4 - my_h, 4)
            for i in range(QUARTERS):
                to_z(v_buf, t_buf, (0,) + quarter(i), h, my_p, last_s.at[i], last_r.at[i])

        t_buf[0, my_p, my_h] = v_buf[0, my_p, my_h]

    for g in range(2):
        wait_hop(0, 1, g, forth)
        hop(1, fx_buf, fy_buf, 1, g, forth)
    for g in range(2):
        wait_hop(1, 1, g, forth)
        send_core(fy_buf, q_buf, 1, g, fc_s, fc_r)
    for g in range(2):
        forward_1(g)
    for half in range(2):
        for g in range(2):
            send_z(q_buf, w_buf, (1, half), g, half_s.at[0, half, g], half_r.at[0, half, g])
    w_buf[1, my_p, my_h] = q_buf[1, my_p, my_h]
    for g in range(2):
        wait_z(q_buf, (0,), g, z_r.at[g])
        rotate_bw(q_buf, 0, g, 0)
        hop(0, q_buf, fx_buf, 0, g, forth)
    for g in range(2):
        wait_hop(0, 0, g, forth)
        hop(1, fx_buf, fy_buf, 0, g, forth)

    def turn_1(half):
        for g in range(2):
            wait_z(w_buf, (1, half), g, half_r.at[0, half, g])
        middle_z(half)
        for g in range(2):
            send_z(m_buf, r_buf, (1, half), g, half_s.at[1, half, g], half_r.at[1, half, g])

    turn_1(0)
    for g in range(2):
        wait_hop(1, 0, g, forth)
        send_core(fy_buf, w_buf, 0, g, fc_s, fc_r)
    for g in range(2):
        wait_w(0, g, fc_r, 2)
    middle(0)
    for g in range(2):
        hop(0, m_buf, bx_buf, 0, g, home)
    turn_1(1)
    r_buf[1, my_p, my_h] = m_buf[1, my_p, my_h]
    for g in range(2):
        wait_hop(0, 0, g, home)
        hop(1, bx_buf, by_buf, 0, g, home)
    for g in range(2):
        wait_hop(1, 0, g, home)
        send_core(by_buf, v_buf, 0, g, bc_s, bc_r)
    for g in range(2):
        back_0(g)
    for half in range(2):
        for g in range(2):
            wait_z(r_buf, (1, half), g, half_r.at[1, half, g])
    for g in range(2):
        rows_and_lanes(r_buf, g, 1)
        hop(0, r_buf, bx_buf, 1, g, home)
    for g in range(2):
        wait_hop(0, 1, g, home)
        hop(1, bx_buf, by_buf, 1, g, home)
    for g in range(2):
        wait_hop(1, 1, g, home)
        send_core(by_buf, t_buf, 1, g, bc_s, bc_r)
    for g in range(2):
        wait_w(1, g, bc_r, 2)
        rotate_bw(t_buf, 1, g, 1)

    second = [gate(1, q) for q in (10, 16, 17, 18)]
    sub = lax.broadcasted_iota(jnp.int32, (8, 128), 0)
    lane = lax.broadcasted_iota(jnp.int32, (8, 128), 1)
    base = ladder(lane, 7) + (lane >> 6 & sub & 1) + ladder(sub, 3)
    base = base + ladder(dev, 5) + ladder(grp, 3) + (dev >> 4 & grp & 1)
    tile_signs = [signs(base + c * (sub >> 2 & 1)) for c in range(2)]
    wait_z(t_buf, (0,), 0, z_r.at[2])
    for i in range(QUARTERS):
        wait_z(t_buf, (0,) + quarter(i), 1, last_r.at[i])

        @pl.loop(8 * i, 8 * i + 8)
        def _(bw):
            place = at_w(bw)
            tiles = [t_buf[(j & 1, j >> 1 & 1, j >> 2) + place] for j in range(16)]
            for bit in range(4):
                tiles = rotate(tiles, bit, second[bit])
            for j in range(16):
                c, z = j & 1, j >> 1
                odd = ladder(bw, 5) + (c & bw & 1) + (bw >> 4 & z & 1) + (z >> 2 & core & 1)
                odd = odd + (z & z >> 1 & 1) + (z >> 1 & z >> 2 & 1)
                out[z, bw, c] = tiles[j] * (tile_signs[c] * signs(odd))

    for g in range(2):
        wait_z(p_buf, (0,), g, z_s.at[g])
        for half in range(2):
            for way in range(2):
                wait_z(r_buf, (1, half), g, half_s.at[way, half, g])
        for c in range(2):
            for sem, n in ((fx_s, 3), (fy_s, 3), (fc_s, 2), (bx_s, 3), (by_s, 3), (bc_s, 2)):
                wait_w(c, g, sem, n)
    wait_z(v_buf, (0,), 0, z_s.at[2])
    for i in range(QUARTERS):
        wait_z(v_buf, (0,) + quarter(i), 1, last_s.at[i])


def shards(state, angles):
    view = (8, 32, 2, 8, 128)
    by_z = (2, 2, 4, 2, 4, 2, 2, 8, 128)
    pairs = pltpu.SemaphoreType.DMA((2, 2))
    quarters = pltpu.SemaphoreType.DMA((QUARTERS,))
    out = pl.pallas_call(
        kernel,
        out_shape=jax.ShapeDtypeStruct(view, F32),
        in_specs=[pl.BlockSpec(memory_space=pltpu.HBM)] * 2,
        out_specs=pl.BlockSpec(memory_space=pltpu.VMEM),
        scratch_shapes=[
            pltpu.VMEM(view, F32), pltpu.VMEM((2, 27), F32),
            *[pltpu.VMEM(by_z, F32)] * 11,
            pltpu.VMEM((4, 256, 256), F32),
            pltpu.VMEM((2, 4, 256, 256), F32),
            pltpu.VMEM((2, 512, 256), BF16), pltpu.VMEM((2, 2, 256, 256), BF16), pltpu.VMEM((2, 2, 256, 256), BF16),
            quarters, pltpu.SemaphoreType.DMA,
            pltpu.SemaphoreType.DMA((3,)), pltpu.SemaphoreType.DMA((3,)),
            pltpu.SemaphoreType.DMA((2, 2, 2)), pltpu.SemaphoreType.DMA((2, 2, 2)),
            quarters, quarters,
            *[pairs] * 12,
        ],
        compiler_params=pltpu.CompilerParams(
            collective_id=0, has_side_effects=True, vmem_limit_bytes=50 * 2**20
        ),
    )(state.reshape(view), angles)
    return out.reshape(state.shape)


def solution(mesh):
    placed = (P("grp", "dev", None), P())
    return jax.shard_map(
        shards, mesh=mesh, in_specs=placed, out_specs=P("grp", "dev", None), check_vma=False
    )
```

```python
import jax
import jax.numpy as jnp
from jax import lax
from jax.experimental import pallas as pl
from jax.experimental.pallas import tpu as pltpu
from jax.sharding import PartitionSpec as P

MESH = pl.DeviceIdType.MESH
F32, BF16 = jnp.float32, jnp.bfloat16
W_QUBITS = (19, 23, 24, 25, 26)
BW_QUBITS = (11, 12, 13, 14, 15)
ROW_QUBITS = (7, 8, 9) + W_QUBITS
COL_QUBITS = (0, 1, 2, 3, 4, 5, 6, 20)
QUARTERS = 4


def rotate(tiles, bit, gate):
    cosine, sine = gate
    out = list(tiles)
    for i in range(len(tiles)):
        if not i >> bit & 1:
            j = i | 1 << bit
            out[i] = cosine * tiles[i] - sine * tiles[j]
            out[j] = sine * tiles[i] + cosine * tiles[j]
    return out


def ladder(values, nbits):
    total = values & values >> 1
    parity = total & 1
    for j in range(1, nbits - 1):
        parity = parity + (total >> j & 1)
    return parity


def signs(parity):
    return (1 - 2 * (parity & 1)).astype(F32)


def split(value):
    high = value.astype(BF16)
    return high, (value - high.astype(F32)).astype(BF16)


def dot3(a, b):
    return (
        jnp.dot(a[0], b[0], preferred_element_type=F32)
        + jnp.dot(a[0], b[1], preferred_element_type=F32)
        + jnp.dot(a[1], b[0], preferred_element_type=F32)
    )


def at_w(w):
    return lax.div(w, 16), lax.rem(lax.div(w, 4), 4), lax.rem(lax.div(w, 2), 2), lax.rem(w, 2)


def kernel(
    state, angles, out,
    x, turns, p_buf, q_buf, w_buf, m_buf, v_buf, t_buf, r_buf, fx_buf, fy_buf, bx_buf, by_buf, ys, cz,
    gate_left, gate_right, gate_lane,
    load_sem, turns_sem, z_s, z_r, half_s, half_r, last_s, last_r, fx_s, fx_r, fy_s, fy_r, fc_s, fc_r, bx_s, bx_r, by_s, by_r, bc_s, bc_r,
):
    grp, dev = lax.axis_index("grp"), lax.axis_index("dev")
    core, my_z, x_lo = lax.rem(dev, 2), lax.rem(lax.div(dev, 2), 8), lax.div(dev, 16)
    my_y, x_hi = lax.rem(grp, 4), lax.div(grp, 4)
    my_w = core + 2 * x_lo + 4 * grp
    my_p, my_h = lax.rem(my_z, 2), lax.div(my_z, 2)

    def z_device(z):
        return (grp, 16 * x_lo + 2 * z + core)

    def x_peer(k):
        there = lax.rem(2 * x_hi + x_lo + k, 4)
        return lax.div(there, 2), lax.rem(there, 2)

    def x_device(hi, lo):
        return (4 * hi + my_y, 16 * lo + 2 * my_z + core)

    def y_device(y):
        return (4 * x_hi + y, dev)

    core_device = (grp, dev + 1 - 2 * core)

    def load(i):
        part = pl.ds(8 * i, 8)
        return pltpu.make_async_copy(state.at[:, part], x.at[:, part], load_sem.at[i])

    load_turns = pltpu.make_async_copy(angles, turns, turns_sem)
    load_turns.start()
    for i in range(QUARTERS):
        load(i).start()
    barrier = pltpu.get_barrier_semaphore()

    @pl.loop(1, 8)
    def _(k):
        pl.semaphore_signal(barrier, inc=1, device_id=z_device(lax.rem(my_z + k, 8)), device_id_type=MESH)

    @pl.loop(1, 4)
    def _(k):
        pl.semaphore_signal(barrier, inc=1, device_id=x_device(*x_peer(k)), device_id_type=MESH)
        pl.semaphore_signal(barrier, inc=1, device_id=y_device(lax.rem(my_y + k, 4)), device_id_type=MESH)

    pl.semaphore_signal(barrier, inc=1, device_id=core_device, device_id_type=MESH)

    load_turns.wait()
    half = 0.5 * turns[...]
    cosines, sines = jnp.cos(half), jnp.sin(half)

    def gate(layer, qubit, shape=(8, 128)):
        at = (slice(layer, layer + 1), slice(qubit, qubit + 1))
        return jnp.broadcast_to(cosines[at], shape), jnp.broadcast_to(sines[at], shape)

    first = [gate(0, q) for q in (10, 16, 17, 18)]
    def quarter(i):
        return i >> 1, pl.ds(2 * (i & 1), 2)

    def parity(g):
        return 1 - my_p if g == 0 else my_p

    def to_z(source, target, place, h, p, send_sem, recv_sem):
        pltpu.make_async_remote_copy(
            src_ref=source.at[(place[0], p, h) + place[1:]], dst_ref=target.at[(place[0], my_p, my_h) + place[1:]],
            send_sem=send_sem, recv_sem=recv_sem, device_id=z_device(2 * h + p), device_id_type=MESH,
        ).start()

    def send_z(source, target, place, g, send_sem, recv_sem):
        if g == 0:
            @pl.loop(0, 4)
            def _(h):
                to_z(source, target, place, h, 1 - my_p, send_sem, recv_sem)
        else:
            @pl.loop(0, 3)
            def _(k):
                to_z(source, target, place, k + lax.div(k + 4 - my_h, 4), my_p, send_sem, recv_sem)

    def wait_z(buffer, place, g, sem):
        part = buffer.at[(place[0], 0, pl.ds(0, 4 - g)) + place[1:]]
        pltpu.make_async_copy(part, part, sem).wait()

    def send_x(source, target, c, g, send_sem, recv_sem):
        p = parity(g)

        @pl.loop(1, 4)
        def _(k):
            hi, lo = x_peer(k)
            pltpu.make_async_remote_copy(
                src_ref=source.at[c, p, :, hi, :, lo], dst_ref=target.at[c, p, :, x_hi, :, x_lo],
                send_sem=send_sem.at[c, g], recv_sem=recv_sem.at[c, g],
                device_id=x_device(hi, lo), device_id_type=MESH,
            ).start()

        target[c, p, :, x_hi, :, x_lo] = source[c, p, :, x_hi, :, x_lo]

    def send_y(source, target, c, g, send_sem, recv_sem):
        p = parity(g)

        @pl.loop(1, 4)
        def _(k):
            y = lax.rem(my_y + k, 4)
            pltpu.make_async_remote_copy(
                src_ref=source.at[c, p, :, :, y], dst_ref=target.at[c, p, :, :, my_y],
                send_sem=send_sem.at[c, g], recv_sem=recv_sem.at[c, g],
                device_id=y_device(y), device_id_type=MESH,
            ).start()

        target[c, p, :, :, my_y] = source[c, p, :, :, my_y]

    def send_core(source, target, c, g, send_sem, recv_sem):
        p = parity(g)
        pltpu.make_async_remote_copy(
            src_ref=source.at[c, p, :, :, :, :, 1 - core], dst_ref=target.at[c, p, :, :, :, :, core],
            send_sem=send_sem.at[c, g], recv_sem=recv_sem.at[c, g],
            device_id=core_device, device_id_type=MESH,
        ).start()
        target[c, p, :, :, :, :, core] = source[c, p, :, :, :, :, core]

    def wait_w(c, g, sem, n=3):
        part = t_buf.at[0, 0, pl.ds(0, n)]
        pltpu.make_async_copy(part, part, sem.at[c, g]).wait()

    def hop(n, source, target, c, g, sems):
        if (n + g) % 2 == 0:
            send_x(source, target, c, g, sems[0], sems[1])
        else:
            send_y(source, target, c, g, sems[2], sems[3])

    def wait_hop(n, c, g, sems):
        wait_w(c, g, sems[1] if (n + g) % 2 == 0 else sems[3])

    forth, home = (fx_s, fx_r, fy_s, fy_r), (bx_s, bx_r, by_s, by_r)

    def rotate_bw(buffer, c, g, layer):
        gates = [gate(layer, q) for q in BW_QUBITS]
        p = parity(g)

        @pl.loop(0, 4)
        def _(h):
            spots = [(c, p, h, w >> 4, w >> 2 & 3, w >> 1 & 1, w & 1) for w in range(32)]
            tiles = [buffer[spot] for spot in spots]
            for bit in range(5):
                tiles = rotate(tiles, bit, gates[bit])
            for spot, tile in zip(spots, tiles):
                buffer[spot] = tile

    for i in range(QUARTERS):
        load(i).wait()

        @pl.loop(8 * i, 8 * i + 8)
        def _(bw):
            tiles = [x[j >> 1, bw, j & 1] for j in range(16)]
            place = at_w(bw)
            for bit in range(4):
                tiles = rotate(tiles, bit, first[bit])
            for j in range(16):
                z = j >> 1
                p_buf[(j & 1, z & 1, z >> 1) + place] = tiles[j]

        if i == 0:
            pl.semaphore_wait(barrier, 14)
        for g in range(2):
            send_z(p_buf, q_buf, (0,) + quarter(i), g, z_s.at[g], z_r.at[g])

    for g in range(2):
        rotate_bw(p_buf, 1, g, 0)
        hop(0, p_buf, fx_buf, 1, g, forth)
    q_buf[0, my_p, my_h] = p_buf[0, my_p, my_h]

    square = (256, 256)
    rows = lax.broadcasted_iota(jnp.int32, square, 0)
    cols = lax.broadcasted_iota(jnp.int32, square, 1)
    for layer in range(2):
        for side, qubits in enumerate((ROW_QUBITS, COL_QUBITS)):
            matrix = None
            for j, q in enumerate(qubits):
                cosine, sine = gate(layer, q, square)
                to, of = (rows, cols) if side == 0 else (cols, rows)
                a, b = to >> j & 1, of >> j & 1
                entry = jnp.where(a == b, cosine, jnp.where(a == 1, sine, -sine))
                lanes = jnp.where(a == b, matrix, 0.0) if j == 7 else None
                matrix = entry if matrix is None else matrix * entry
            high, low = split(matrix)
            if side == 0:
                gate_left[layer, :256], gate_left[layer, 256:] = high, low
            else:
                gate_right[layer, 0], gate_right[layer, 1] = high, low
                gate_lane[layer, 0], gate_lane[layer, 1] = split(lanes)

    w_row, p_col = rows >> 3, cols >> 7
    fixed = ladder(my_w, 5) + ladder(my_z, 3) + (my_w >> 4 & my_z & 1)
    cross = (
        ladder(cols & 127, 7) + (cols >> 6 & rows & 1) + ladder(rows & 7, 3) + (my_z >> 2 & w_row & 1)
        + (w_row & p_col & 1) + ladder(w_row >> 1, 4) + fixed
    )
    for h in range(4):
        with_h = cross + (p_col & h & 1) + (h >> 1 & w_row >> 1 & 1) + (h & h >> 1 & 1)
        cz[0, h] = signs(with_h)
        cz[1, h] = signs(with_h + (rows >> 2 & 1) + (my_w & 1))

    h_gates = [[gate(layer, q, (32, 256)) for q in (21, 22)] for layer in range(2)]

    def left(layer, block):
        high, low = split(block)
        both = jnp.dot(gate_left[layer], high, preferred_element_type=F32)
        return both[:256] + both[256:] + jnp.dot(gate_left[layer, :256], low, preferred_element_type=F32)

    def right(gates, layer, block):
        high, low = split(block)
        both = jnp.dot(jnp.concatenate([high, low], axis=0), gates[layer, 0], preferred_element_type=F32)
        return both[:256] + both[256:] + jnp.dot(high, gates[layer, 1], preferred_element_type=F32)

    def rows_and_lanes(buffer, g, layer):
        p = parity(g)
        for h in (0, 2):
            block = jnp.concatenate([buffer[1, p, h + i].reshape(256, 128) for i in range(2)], axis=1)
            block = right(gate_lane, layer, left(layer, block))
            for i in range(2):
                buffer[1, p, h + i] = block[:, 128 * i:128 * i + 128].reshape(2, 4, 2, 2, 8, 128)

    z_gates = [[gate(layer, q) for q in (20, 21, 22)] for layer in range(2)]

    def middle_z(half):
        @pl.loop(0, 16)
        def _(k):
            w = 16 * half + k
            place = at_w(w)
            tiles = [w_buf[(1, z & 1, z >> 1) + place] for z in range(8)]
            for bit in range(3):
                tiles = rotate(tiles, bit, z_gates[0][bit])
            part = pl.ds(pl.multiple_of(8 * w, 8), 8)
            for z in range(8):
                tiles[z] = tiles[z] * cz[1, z >> 1, part, 128 * (z & 1):128 * (z & 1) + 128]
            for bit in range(3):
                tiles = rotate(tiles, bit, z_gates[1][bit])
            for z in range(8):
                m_buf[(1, z & 1, z >> 1) + place] = tiles[z]

    def middle(c):
        for h in range(4):
            block = jnp.concatenate([w_buf[c, p, h].reshape(256, 128) for p in range(2)], axis=1)
            ys[h] = right(gate_right, 0, left(0, block))

        @pl.loop(0, 8)
        def _(r):
            part = pl.ds(pl.multiple_of(32 * r, 32), 32)
            tiles = [ys[h, part] for h in range(4)]
            for layer in range(2):
                for bit in range(2):
                    tiles = rotate(tiles, bit, h_gates[layer][bit])
                if layer == 0:
                    tiles = [tiles[h] * cz[c, h, part] for h in range(4)]
            for h in range(4):
                ys[h, part] = tiles[h]

        for h in range(4):
            block = right(gate_right, 1, left(1, ys[h]))
            for p in range(2):
                m_buf[c, p, h] = block[:, 128 * p:128 * p + 128].reshape(2, 4, 2, 2, 8, 128)

    def forward_1(g):
        wait_w(1, g, fc_r, 2)
        rows_and_lanes(q_buf, g, 0)

    def back_0(g):
        wait_w(0, g, bc_r, 2)
        rotate_bw(v_buf, 0, g, 1)
        if g == 0:
            send_z(v_buf, t_buf, (0,), 0, z_s.at[2], z_r.at[2])
            return

        for i in range(QUARTERS):
            send_z(v_buf, t_buf, (0,) + quarter(i), 1, last_s.at[i], last_r.at[i])
        t_buf[0, my_p, my_h] = v_buf[0, my_p, my_h]

    for g in range(2):
        wait_hop(0, 1, g, forth)
        hop(1, fx_buf, fy_buf, 1, g, forth)
    for g in range(2):
        wait_hop(1, 1, g, forth)
        send_core(fy_buf, q_buf, 1, g, fc_s, fc_r)
    for g in range(2):
        forward_1(g)
    for half in range(2):
        for g in range(2):
            send_z(q_buf, w_buf, (1, half), g, half_s.at[0, half, g], half_r.at[0, half, g])
    w_buf[1, my_p, my_h] = q_buf[1, my_p, my_h]
    for g in range(2):
        wait_z(q_buf, (0,), g, z_r.at[g])
        rotate_bw(q_buf, 0, g, 0)
        hop(0, q_buf, fx_buf, 0, g, forth)
    for g in range(2):
        wait_hop(0, 0, g, forth)
        hop(1, fx_buf, fy_buf, 0, g, forth)

    def turn_1(half):
        for g in range(2):
            wait_z(w_buf, (1, half), g, half_r.at[0, half, g])
        middle_z(half)
        for g in range(2):
            send_z(m_buf, r_buf, (1, half), g, half_s.at[1, half, g], half_r.at[1, half, g])

    turn_1(0)
    for g in range(2):
        wait_hop(1, 0, g, forth)
        send_core(fy_buf, w_buf, 0, g, fc_s, fc_r)
    for g in range(2):
        wait_w(0, g, fc_r, 2)
    middle(0)
    for g in range(2):
        hop(0, m_buf, bx_buf, 0, g, home)
    turn_1(1)
    r_buf[1, my_p, my_h] = m_buf[1, my_p, my_h]
    for g in range(2):
        wait_hop(0, 0, g, home)
        hop(1, bx_buf, by_buf, 0, g, home)
    for g in range(2):
        wait_hop(1, 0, g, home)
        send_core(by_buf, v_buf, 0, g, bc_s, bc_r)
    for g in range(2):
        back_0(g)
    for half in range(2):
        for g in range(2):
            wait_z(r_buf, (1, half), g, half_r.at[1, half, g])
    for g in range(2):
        rows_and_lanes(r_buf, g, 1)
        hop(0, r_buf, bx_buf, 1, g, home)
    for g in range(2):
        wait_hop(0, 1, g, home)
        hop(1, bx_buf, by_buf, 1, g, home)
    for g in range(2):
        wait_hop(1, 1, g, home)
        send_core(by_buf, t_buf, 1, g, bc_s, bc_r)
    for g in range(2):
        wait_w(1, g, bc_r, 2)
        rotate_bw(t_buf, 1, g, 1)

    second = [gate(1, q) for q in (10, 16, 17, 18)]
    sub = lax.broadcasted_iota(jnp.int32, (8, 128), 0)
    lane = lax.broadcasted_iota(jnp.int32, (8, 128), 1)
    base = ladder(lane, 7) + (lane >> 6 & sub & 1) + ladder(sub, 3)
    base = base + ladder(dev, 5) + ladder(grp, 3) + (dev >> 4 & grp & 1)
    tile_signs = [signs(base + c * (sub >> 2 & 1)) for c in range(2)]
    wait_z(t_buf, (0,), 0, z_r.at[2])
    for i in range(QUARTERS):
        wait_z(t_buf, (0,) + quarter(i), 1, last_r.at[i])

        @pl.loop(8 * i, 8 * i + 8)
        def _(bw):
            place = at_w(bw)
            tiles = [t_buf[(j & 1, j >> 1 & 1, j >> 2) + place] for j in range(16)]
            for bit in range(4):
                tiles = rotate(tiles, bit, second[bit])
            for j in range(16):
                c, z = j & 1, j >> 1
                odd = ladder(bw, 5) + (c & bw & 1) + (bw >> 4 & z & 1) + (z >> 2 & core & 1)
                odd = odd + (z & z >> 1 & 1) + (z >> 1 & z >> 2 & 1)
                out[z, bw, c] = tiles[j] * (tile_signs[c] * signs(odd))

    for g in range(2):
        wait_z(p_buf, (0,), g, z_s.at[g])
        for half in range(2):
            for way in range(2):
                wait_z(r_buf, (1, half), g, half_s.at[way, half, g])
        for c in range(2):
            for sem, n in ((fx_s, 3), (fy_s, 3), (fc_s, 2), (bx_s, 3), (by_s, 3), (bc_s, 2)):
                wait_w(c, g, sem, n)
    wait_z(v_buf, (0,), 0, z_s.at[2])
    for i in range(QUARTERS):
        wait_z(v_buf, (0,) + quarter(i), 1, last_s.at[i])


def shards(state, angles):
    view = (8, 32, 2, 8, 128)
    by_z = (2, 2, 4, 2, 4, 2, 2, 8, 128)
    pairs = pltpu.SemaphoreType.DMA((2, 2))
    quarters = pltpu.SemaphoreType.DMA((QUARTERS,))
    out = pl.pallas_call(
        kernel,
        out_shape=jax.ShapeDtypeStruct(view, F32),
        in_specs=[pl.BlockSpec(memory_space=pltpu.HBM)] * 2,
        out_specs=pl.BlockSpec(memory_space=pltpu.VMEM),
        scratch_shapes=[
            pltpu.VMEM(view, F32), pltpu.VMEM((2, 27), F32),
            *[pltpu.VMEM(by_z, F32)] * 11,
            pltpu.VMEM((4, 256, 256), F32),
            pltpu.VMEM((2, 4, 256, 256), F32),
            pltpu.VMEM((2, 512, 256), BF16), pltpu.VMEM((2, 2, 256, 256), BF16), pltpu.VMEM((2, 2, 256, 256), BF16),
            quarters, pltpu.SemaphoreType.DMA,
            pltpu.SemaphoreType.DMA((3,)), pltpu.SemaphoreType.DMA((3,)),
            pltpu.SemaphoreType.DMA((2, 2, 2)), pltpu.SemaphoreType.DMA((2, 2, 2)),
            quarters, quarters,
            *[pairs] * 12,
        ],
        compiler_params=pltpu.CompilerParams(
            collective_id=0, has_side_effects=True, vmem_limit_bytes=50 * 2**20
        ),
    )(state.reshape(view), angles)
    return out.reshape(state.shape)


def solution(mesh):
    placed = (P("grp", "dev", None), P())
    return jax.shard_map(
        shards, mesh=mesh, in_specs=placed, out_specs=P("grp", "dev", None), check_vma=False
    )
```
